128 devices in a mesh: tm: 128 (over y, x, z, core).
Axes of the slice: x: 4, y: 4, z: 4, core: 2. Of those that a mesh axis runs over, the one named last changes fastest.
Arguments:
- filtered_mean: float32 [4096, 192], P('tm'), may hold values from -6 to 6
- filtered_cov: float32 [4096, 192, 192], P('tm'), may hold values from -0.2 to 1.35, as said below
- dynamics: float32 [4096, 192, 192], P('tm'), may hold values from -1 to 1
- predicted_precision: float32 [4096, 192, 192], P('tm'), may hold values from -1 to 2, as said below
Outputs:
- smoothed_state_means: float32 [4096, 192], P('tm')
- smooth_cov: float32 [4096, 192, 192], P('tm')
The draws below stay inside these ranges and needn't reach their ends.
Inputs may be any that keep to these rules, and one draw needn't show every extreme that they name: `filtered_cov`: symmetric in its last two dimensions. `predicted_precision`: symmetric in its last two dimensions; for k >= 1, predicted_precision[k] is the inverse of a covariance that is at least dynamics[k-1] filtered_cov[k-1] dynamics[k-1]^T.
All inputs are finite; a program needn't handle non-finite values.
Results may differ from the reference program's by a relative error of at most 0.0003.
Values sent between devices are 32-bit elements; how exact they have to be, the bound alone decides.
No kernel may reach another device: no remote copies, remote signals or barrier semaphores. Data moves between devices by JAX's collectives and lax.ppermute only.
A program may use at most 192 MiB of HBM per device.

```python
import math
import jax
import jax.numpy as jnp
from jax import lax

D = 192
EPOCH_COUNT = 4096


HIGH = lax.Precision.HIGHEST


def covariance_matrices(key):
    base_key = jax.random.fold_in(key, 11)
    first_key, second_key = jax.random.split(base_key)
    unit_matrix = jnp.eye(D, dtype=jnp.float32)
    normal_part = jax.random.truncated_normal(first_key, -4.0, 4.0, (EPOCH_COUNT, D, D), jnp.float32)
    off_part = (normal_part + jnp.swapaxes(normal_part, 1, 2)) * (0.1 / math.sqrt(2.0 * D)) * (1.0 - unit_matrix)
    diagonal_part = jax.random.uniform(second_key, (EPOCH_COUNT, D), jnp.float32, 0.8, 1.2)
    return off_part + unit_matrix * diagonal_part[:, :, None]


def rotation_matrices(key):
    base_key = jax.random.fold_in(key, 13)
    unit_matrix = jnp.eye(D, dtype=jnp.float32)
    raw_part = jax.random.truncated_normal(base_key, -4.0, 4.0, (EPOCH_COUNT, D, D), jnp.float32)
    skew_part = (raw_part - jnp.swapaxes(raw_part, 1, 2)) * (0.5 / math.sqrt(2.0 * D))
    left_side = unit_matrix - 0.5 * skew_part
    right_side = unit_matrix + 0.5 * skew_part
    return jnp.linalg.solve(left_side, right_side)


def noise_levels(key):
    base_key = jax.random.fold_in(key, 17)
    rate_key, spot_key, discard_random_key = jax.random.split(base_key, 3)
    step_rates = jax.random.uniform(rate_key, (EPOCH_COUNT,), jnp.float32, 0.2, 1.4)
    impulse_length_values = jax.random.uniform(discard_random_key, (3,), jnp.float32, 0.3, 1.0)
    sampled_position_index = jax.random.randint(spot_key, (3,), 0, EPOCH_COUNT - 1)
    position_index_entries = jnp.arange(EPOCH_COUNT, dtype=jnp.int32)
    abrupt_perturbation = jnp.sum(jnp.where(position_index_entries[:, None] == sampled_position_index[None, :], impulse_length_values[None, :], 0.0), axis=1)
    return step_rates / EPOCH_COUNT + abrupt_perturbation


def process_noise(key):
    base_key = jax.random.fold_in(key, 19)
    shape_key, scale_key = jax.random.split(base_key)
    unit_matrix = jnp.eye(D, dtype=jnp.float32)
    normal_part = jax.random.truncated_normal(shape_key, -4.0, 4.0, (EPOCH_COUNT, D, D), jnp.float32)
    off_part = (normal_part + jnp.swapaxes(normal_part, 1, 2)) * (0.1 / math.sqrt(2.0 * D)) * (1.0 - unit_matrix)
    channel_scales = jnp.exp(jax.random.uniform(scale_key, (EPOCH_COUNT, D), jnp.float32, math.log(0.3), math.log(3.0)))
    square_root_scale_factors = jnp.sqrt(channel_scales)
    shape_matrix = (unit_matrix + off_part) * square_root_scale_factors[:, :, None] * square_root_scale_factors[:, None, :]
    return shape_matrix * noise_levels(key)[:, None, None]


def draw_filtered_cov(key, part):
    return covariance_matrices(key)


def draw_dynamics(key, part):
    return rotation_matrices(key)


def draw_predicted_precision(key, part):
    cov_matrices = covariance_matrices(key)
    rotations = rotation_matrices(key)
    left_part = jnp.matmul(rotations, cov_matrices, precision=HIGH)
    predicted_cov = jnp.matmul(left_part, jnp.swapaxes(rotations, 1, 2), precision=HIGH)
    predicted_cov = 0.5 * (predicted_cov + jnp.swapaxes(predicted_cov, 1, 2)) + process_noise(key)
    precision_now = jnp.linalg.inv(predicted_cov)
    precision_now = 0.5 * (precision_now + jnp.swapaxes(precision_now, 1, 2))
    return jnp.roll(precision_now, 1, axis=0)


def level_of(own_key, shape, cuts, low, largest):
    def one(dim, shards_of):
        heights = jax.random.uniform(jax.random.fold_in(jax.random.fold_in(own_key, 6), dim), (shards_of,), jnp.float32, low / len(cuts), largest / len(cuts))
        return jnp.repeat(jnp.exp(heights), shape[dim] // shards_of).reshape((-1,) + (1,) * (len(shape) - dim - 1))

    loudness = one(*cuts[0])
    for cut in cuts[1:]:
        loudness = loudness * one(*cut)
    return loudness


def normal_values(stream_key, dims, scale, limit, shards=(), kind=jnp.bfloat16):
    level = level_of(stream_key, dims, shards, -0.22, 0.18) if shards else 1.0
    array = jax.random.normal(stream_key, dims, jnp.float32) * scale * level
    return jnp.minimum(jnp.maximum(array, -limit), limit).astype(kind)


def setup_inputs(seed: int = 0) -> dict:
    keys = jax.random.split(jax.random.key(seed), 5)
    return {
        "filtered_mean": normal_values(keys[0], (EPOCH_COUNT, D), 1.0, 6.0, ((0, 128),), jnp.float32),
        "filtered_cov": draw_filtered_cov(jax.random.fold_in(keys[4], 71), 0),
        "dynamics": draw_dynamics(jax.random.fold_in(keys[4], 71), 0),
        "predicted_precision": draw_predicted_precision(jax.random.fold_in(keys[4], 71), 0),
    }


HIGH = lax.Precision.HIGHEST

def reference(filtered_mean, filtered_cov, dynamics, predicted_precision):

    def back_step(carry, element):
        mean_next, cov_next = carry
        mean_here, cov_here, dyn_here, prec_next = element
        process_covariance = jnp.einsum('ij,lj->il', cov_here, dyn_here, precision=HIGH)
        gain = jnp.dot(process_covariance, prec_next, precision=HIGH)
        predicted_state = jnp.dot(dyn_here, mean_here, precision=HIGH)
        offset = mean_here - jnp.dot(gain, predicted_state, precision=HIGH)
        dyn_cov = jnp.dot(dyn_here, cov_here, precision=HIGH)
        resid = cov_here - jnp.dot(gain, dyn_cov, precision=HIGH)
        mean_now = jnp.dot(gain, mean_next, precision=HIGH) + offset
        gain_cov = jnp.dot(gain, cov_next, precision=HIGH)
        cov_now = jnp.einsum('ij,mj->im', gain_cov, gain, precision=HIGH) + resid
        return ((mean_now, cov_now), (mean_now, cov_now))
    last_mean = filtered_mean[-1]
    last_cov = filtered_cov[-1]
    scan_element_list = (filtered_mean[:-1], filtered_cov[:-1], dynamics[:-1], predicted_precision[1:])
    final_carry, stacked = lax.scan(back_step, (last_mean, last_cov), scan_element_list, reverse=True)
    means = jnp.concatenate([stacked[0], last_mean[None]], 0)
    covs = jnp.concatenate([stacked[1], last_cov[None]], 0)
    return (means, covs)
```

```python
import jax
import jax.numpy as jnp
from jax import lax
from jax.experimental import pallas as pl
from jax.experimental.pallas import tpu as pltpu
from jax.sharding import PartitionSpec as P

HIGHEST = lax.Precision.HIGHEST
F32 = jnp.float32
W = 192
STEPS = 8
ROWS = 592
HALF = ROWS // 2
VMEM_LIMIT = 60 << 20


def times(a, b):
    return jnp.dot(a, b, precision=HIGHEST, preferred_element_type=F32)


def times_t(a, b):
    return lax.dot_general(
        a, b, (((1,), (1,)), ((), ())), precision=HIGHEST, preferred_element_type=F32
    )


def split(x):
    high = x.astype(jnp.bfloat16)
    return high, (x - high.astype(F32)).astype(jnp.bfloat16)


def three(a, b, side):
    def part(x, y):
        return lax.dot_general(x, y, (((1,), (side,)), ((), ())), preferred_element_type=F32)

    return part(a[0], b[0]) + (part(a[0], b[1]) + part(a[1], b[0]))


def packed(e, l, u, ref):
    ref[0:192, :] = e[:, :128]
    ref[192:384, :] = jnp.concatenate([e[:, 128:], l[:, 128:]], 1)
    ref[384:576, :] = l[:, :128]
    ref[576:592, :] = jnp.zeros((16, 128), F32)
    ref[576:577, :] = u[0:1, :128]
    ref[577:578, 0:64] = u[0:1, 128:]


def unpacked(ref):
    tail = ref[192:384, :]
    e = jnp.concatenate([ref[0:192, :], tail[:, :64]], 1)
    l = jnp.concatenate([ref[384:576, :], tail[:, 64:]], 1)
    u = jnp.concatenate([ref[576:577, :], ref[577:578, 0:64]], 1)
    return e, l, jnp.broadcast_to(u, (16, W))


def applied(e, l, u, cov, mean):
    left = three(e, cov, 0)
    both = three(split(jnp.concatenate([left, mean], 0)), e, 1)
    return both[:W] + l, both[W:] + u


def composed(first, second):
    e = split(first[0])
    l, u = applied(e, first[1], first[2], split(second[1]), second[2])
    return three(e, split(second[0]), 0), l, u


def in_three(rows):
    high = rows.astype(jnp.bfloat16).astype(F32)
    rest = rows - high
    middle = rest.astype(jnp.bfloat16).astype(F32)
    at = lax.broadcasted_iota(jnp.int32, (16, W), 0)
    tail = jnp.where(at == 2, rest - middle, 0.0)
    return jnp.where(at == 0, high, jnp.where(at == 1, middle, tail))


def eye():
    return (
        lax.broadcasted_iota(jnp.int32, (W, W), 0) == lax.broadcasted_iota(jnp.int32, (W, W), 1)
    ).astype(F32)


def cross_kernel(mean, cov, dyn, cross, moved):
    for j in range(STEPS):
        rows = jnp.concatenate([cov[j], jnp.broadcast_to(mean[j : j + 1], (8, W))], 0)
        both = times_t(rows, dyn[j])
        cross[j] = both[:W]
        moved[j : j + 1] = both[W : W + 1]


def fold_kernel(
    following, mean, cov, cross, moved, precision, e_out, l_out, u_out, total, nxt, e_now, l_now, u_now
):
    @pl.when(pl.program_id(0) == 0)
    def _():
        nxt[...] = following[0]
        e_now[...] = eye()
        l_now[...] = jnp.zeros((W, W), F32)
        u_now[...] = jnp.zeros((16, W), F32)

    def element(j):
        after = nxt[...] if j == STEPS - 1 else precision[j + 1]
        gain = times(cross[j], after)
        return gain, cov[j] - times_t(gain, cross[j])

    e, l, u = e_now[...], l_now[...], u_now[...]
    ready = element(STEPS - 1)
    for j in reversed(range(STEPS)):
        gain, resid = ready
        if j:
            ready = element(j - 1)
        gain_split = split(gain)
        left = three(gain_split, split(l), 0)
        e = times(gain, e)
        rows = jnp.concatenate([left, in_three(u - moved[j : j + 1])], 0)
        both = three(split(rows), gain_split, 1)
        l = both[:W] + resid
        u = jnp.broadcast_to(jnp.sum(both[W:], 0, keepdims=True) + mean[j : j + 1], (16, W))
        e_out[j] = e
        l_out[j] = l
        u_out[j : j + 1] = u[0:1]
    nxt[...] = precision[0]
    e_now[...] = e
    l_now[...] = l
    u_now[...] = u

    @pl.when(pl.program_id(0) == pl.num_programs(0) - 1)
    def _():
        packed(e_now[...], l_now[...], u_now[...], total)


def pair_kernel(place, own, other, total, half, after):
    low = place[1] == 0

    @pl.when(low)
    def _():
        after[...] = other[...]
        packed(*composed(unpacked(own), unpacked(other)), total)

    @pl.when(jnp.logical_not(low))
    def _():
        packed(eye(), jnp.zeros((W, W), F32), jnp.zeros((16, W), F32), after)
        packed(*composed(unpacked(other), unpacked(own)), total)

    half[...] = total[pl.ds(pl.multiple_of(place[1] * HALF, 8), HALF), :]


def arrange(place, own, halves, ordered):
    spot, core = place[0], place[1]
    ordered[spot] = own[...]
    mine = pl.multiple_of(core * HALF, 8)
    theirs = pl.multiple_of((1 - core) * HALF, 8)
    for k in range(3):
        slot = lax.rem(spot + k + 1, 4)
        ordered[slot, pl.ds(mine, HALF), :] = halves[2 * k][...]
        ordered[slot, pl.ds(theirs, HALF), :] = halves[2 * k + 1][...]


def quad_kernel(place, own, *refs):
    halves, (total, half, ordered) = refs[:6], refs[6:]
    arrange(place, own, halves, ordered)
    parts = [unpacked(ordered.at[k]) for k in range(4)]
    early, late = composed(parts[0], parts[1]), composed(parts[2], parts[3])
    packed(*composed(early, late), total)
    half[...] = total[pl.ds(pl.multiple_of(place[1] * HALF, 8), HALF), :]


def join_kernel(place, near, own, *refs):
    halves, (joined, ordered) = refs[:6], refs[6:]
    arrange(place, own, halves, ordered)
    joined[...] = near[...]
    for k in (1, 2, 3):

        @pl.when(k > place[0])
        def _():
            packed(*composed(unpacked(joined), unpacked(ordered.at[k])), joined)


def advance(element, cov, mean):
    e, l, u = unpacked(element)
    cov[...], mean[...] = applied(split(e), l, u, split(cov[...]), mean[...])


def finish_kernel(place, near, own, *refs):
    halves, (e_all, l_all, u_all, mean_out, cov_out, ordered, cov_in, mean_in) = refs[:6], refs[6:]

    @pl.when(pl.program_id(0) == 0)
    def _():
        arrange(place, own, halves, ordered)
        cov_in[...] = jnp.zeros((W, W), F32)
        mean_in[...] = jnp.zeros((16, W), F32)
        for k in (3, 2, 1):

            @pl.when(k > place[0])
            def _():
                advance(ordered.at[k], cov_in, mean_in)

        advance(near, cov_in, mean_in)

    cov, mean = split(cov_in[...]), mean_in[...]
    for j in range(STEPS):
        now, u = applied(split(e_all[j]), l_all[j], u_all[j : j + 1], cov, mean)
        cov_out[j] = now
        mean_out[j : j + 1] = u[0:1]


def struct(*shape):
    return jax.ShapeDtypeStruct(shape, F32)


def cost(products, passes, size):
    return pl.CostEstimate(
        flops=products * passes * 2 * W**3, bytes_accessed=size, transcendentals=0
    )


PARAMS = pltpu.CompilerParams(vmem_limit_bytes=VMEM_LIMIT)
WHOLE = pl.BlockSpec(memory_space=pltpu.VMEM)
SCALAR = pl.BlockSpec(memory_space=pltpu.SMEM)
ELEMENT = ROWS * 128 * 4


def on_device(filtered_mean, filtered_cov, dynamics, predicted_precision):
    peers = lax.axis_size("tm")
    here = lax.axis_index("tm")
    count = filtered_mean.shape[0]
    blocks = count // STEPS
    matrices = count * W * 256 * 4

    following = lax.ppermute(
        predicted_precision[:1], "tm", [(i, i - 1) for i in range(1, peers)]
    )

    up = lambda i: (i, 0)
    up3 = lambda i: (i, 0, 0)
    vec, mat = pl.BlockSpec((STEPS, W), up), pl.BlockSpec((STEPS, W, W), up3)
    cross, moved = pl.pallas_call(
        cross_kernel,
        grid=(blocks,),
        in_specs=[vec, mat, mat],
        out_specs=[mat, vec],
        out_shape=[struct(count, W, W), struct(count, W)],
        compiler_params=PARAMS,
        cost_estimate=cost(count, 6, 3 * matrices),
        name="cross",
    )(filtered_mean, filtered_cov, dynamics)

    down = pl.BlockSpec((STEPS, W), lambda i: (blocks - 1 - i, 0))
    down3 = pl.BlockSpec((STEPS, W, W), lambda i: (blocks - 1 - i, 0, 0))
    once = pl.BlockSpec((1, W, W), lambda i: (0, 0, 0))
    e_all, l_all, u_all, total = pl.pallas_call(
        fold_kernel,
        grid=(blocks,),
        in_specs=[once, down, down3, down3, down, down3],
        out_specs=[down3, down3, down, pl.BlockSpec((ROWS, 128), lambda i: (0, 0))],
        out_shape=[struct(count, W, W), struct(count, W, W), struct(count, W), struct(ROWS, 128)],
        scratch_shapes=[
            pltpu.VMEM((W, W), F32),
            pltpu.VMEM((W, W), F32),
            pltpu.VMEM((W, W), F32),
            pltpu.VMEM((16, W), F32),
        ],
        compiler_params=PARAMS,
        cost_estimate=cost(5 * count, 6, 5 * matrices),
        name="fold",
    )(following, filtered_mean, filtered_cov, cross, moved, predicted_precision)

    def place(stride):
        return jnp.stack([lax.rem(lax.div(here, stride), 4), lax.rem(here, 2)])

    def other_core(part):
        return lax.ppermute(part, "tm", [(i, i ^ 1) for i in range(peers)])

    total, half, near = pl.pallas_call(
        pair_kernel,
        in_specs=[SCALAR, WHOLE, WHOLE],
        out_specs=[WHOLE] * 3,
        out_shape=[struct(ROWS, 128), struct(HALF, 128), struct(ROWS, 128)],
        compiler_params=PARAMS,
        cost_estimate=cost(3, 3, 4 * ELEMENT),
        name="pair",
    )(place(1), total, other_core(total))

    def gathered(half, stride, later_only):
        got = [None] * 3
        for k in (2, 1, 3):
            pairs = []
            for i in range(peers):
                spot = i // stride % 4
                if spot + k < 4 or not later_only:
                    pairs.append((i + ((spot + k) % 4 - spot) * stride, i))
            mine = lax.ppermute(half, "tm", pairs)
            got[k - 1] = (mine, other_core(mine))
        return [part for two in got for part in two]

    for stride in (2, 8):
        parts = gathered(half, stride, False)
        own = total
        total, half = pl.pallas_call(
            quad_kernel,
            in_specs=[SCALAR] + [WHOLE] * 7,
            out_specs=[WHOLE, WHOLE],
            out_shape=[struct(ROWS, 128), struct(HALF, 128)],
            scratch_shapes=[pltpu.VMEM((4, ROWS, 128), F32)],
            compiler_params=PARAMS,
            cost_estimate=cost(9, 3, 6 * ELEMENT),
            name="quad",
        )(place(stride), own, *parts)
        near = pl.pallas_call(
            join_kernel,
            in_specs=[SCALAR] + [WHOLE] * 8,
            out_specs=WHOLE,
            out_shape=struct(ROWS, 128),
            scratch_shapes=[pltpu.VMEM((4, ROWS, 128), F32)],
            compiler_params=PARAMS,
            cost_estimate=cost(9, 3, 6 * ELEMENT),
            name="join",
        )(place(stride), near, own, *parts)

    parts = gathered(half, 32, True)
    flat = pl.BlockSpec((ROWS, 128), lambda i: (0, 0))
    flat_half = pl.BlockSpec((HALF, 128), lambda i: (0, 0))
    return pl.pallas_call(
        finish_kernel,
        grid=(blocks,),
        in_specs=[SCALAR] + [flat] * 2 + [flat_half] * 6 + [mat, mat, vec],
        out_specs=[vec, mat],
        out_shape=[struct(count, W), struct(count, W, W)],
        scratch_shapes=[
            pltpu.VMEM((4, ROWS, 128), F32),
            pltpu.VMEM((W, W), F32),
            pltpu.VMEM((16, W), F32),
        ],
        compiler_params=PARAMS,
        cost_estimate=cost(2 * count, 3, 3 * matrices),
        name="finish",
    )(place(32), near, total, *parts, e_all, l_all, u_all)


def solution(mesh):
    in_specs = (P("tm", None), P("tm", None, None), P("tm", None, None), P("tm", None, None))
    out_specs = (P("tm", None), P("tm", None, None))
    return jax.shard_map(
        lambda *args: tuple(on_device(*args)),
        mesh=mesh,
        in_specs=in_specs,
        out_specs=out_specs,
        check_vma=False,
    )
```

```python
import functools

import jax
import jax.numpy as jnp
from jax import lax
from jax.experimental import pallas as pl
from jax.experimental.pallas import tpu as pltpu
from jax.sharding import PartitionSpec as P

HIGHEST = lax.Precision.HIGHEST
F32 = jnp.float32
W = 192
STEPS = 8
ROWS = 592
HALF = ROWS // 2
VMEM_LIMIT = 60 << 20


def times(a, b):
    return jnp.dot(a, b, precision=HIGHEST, preferred_element_type=F32)


def times_t(a, b):
    return lax.dot_general(
        a, b, (((1,), (1,)), ((), ())), precision=HIGHEST, preferred_element_type=F32
    )


def split(x):
    high = x.astype(jnp.bfloat16)
    return high, (x - high.astype(F32)).astype(jnp.bfloat16)


def filled(x, dim):
    shape = list(x.shape)
    shape[dim] = 256 - W
    return jnp.concatenate([x, jnp.zeros(shape, x.dtype)], dim)


def three(a, b, side):
    high, low = filled(a[0], 1), filled(a[1], 1)
    left = jnp.concatenate([high, high, low], 1)
    high, low = filled(b[0], side), filled(b[1], side)
    right = jnp.concatenate([high, low, high], side)
    return lax.dot_general(left, right, (((1,), (side,)), ((), ())), preferred_element_type=F32)


def packed(e, l, u, ref):
    ref[0:192, :] = e[:, :128]
    ref[192:384, :] = jnp.concatenate([e[:, 128:], l[:, 128:]], 1)
    ref[384:576, :] = l[:, :128]
    ref[576:592, :] = jnp.zeros((16, 128), F32)
    ref[576:577, :] = u[0:1, :128]
    ref[577:578, 0:64] = u[0:1, 128:]


def unpacked(ref):
    tail = ref[192:384, :]
    e = jnp.concatenate([ref[0:192, :], tail[:, :64]], 1)
    l = jnp.concatenate([ref[384:576, :], tail[:, 64:]], 1)
    u = jnp.concatenate([ref[576:577, :], ref[577:578, 0:64]], 1)
    return e, l, jnp.broadcast_to(u, (16, W))


def applied(e, l, u, cov, mean):
    left = three(e, cov, 0)
    both = three(split(jnp.concatenate([left, mean], 0)), e, 1)
    return both[:W] + l, both[W:] + u


def composed(first, second):
    e = split(first[0])
    l, u = applied(e, first[1], first[2], split(second[1]), second[2])
    return three(e, split(second[0]), 0), l, u


def in_three(rows):
    high = rows.astype(jnp.bfloat16).astype(F32)
    rest = rows - high
    middle = rest.astype(jnp.bfloat16).astype(F32)
    at = lax.broadcasted_iota(jnp.int32, (16, W), 0)
    tail = jnp.where(at == 2, rest - middle, 0.0)
    return jnp.where(at == 0, high, jnp.where(at == 1, middle, tail))


def eye():
    return (
        lax.broadcasted_iota(jnp.int32, (W, W), 0) == lax.broadcasted_iota(jnp.int32, (W, W), 1)
    ).astype(F32)


def cross_kernel(mean, cov, dyn, cross, moved):
    for j in range(STEPS):
        rows = jnp.concatenate([cov[j], jnp.broadcast_to(mean[j : j + 1], (8, W))], 0)
        both = times_t(rows, dyn[j])
        cross[j] = both[:W]
        moved[j : j + 1] = both[W : W + 1]


def fold_kernel(
    following, mean, cov, cross, moved, precision, e_out, l_out, u_out, total, nxt, e_now, l_now, u_now
):
    @pl.when(pl.program_id(0) == 0)
    def _():
        nxt[...] = following[0]
        e_now[...] = eye()
        l_now[...] = jnp.zeros((W, W), F32)
        u_now[...] = jnp.zeros((16, W), F32)

    def element(j):
        after = nxt[...] if j == STEPS - 1 else precision[j + 1]
        gain = times(cross[j], after)
        return gain, cov[j] - times_t(gain, cross[j])

    e, l, u = e_now[...], l_now[...], u_now[...]
    ready = element(STEPS - 1)
    for j in reversed(range(STEPS)):
        gain, resid = ready
        if j:
            ready = element(j - 1)
        gain_split = split(gain)
        left = three(gain_split, split(l), 0)
        e = times(gain, e)
        rows = jnp.concatenate([left, in_three(u - moved[j : j + 1])], 0)
        both = three(split(rows), gain_split, 1)
        l = both[:W] + resid
        u = jnp.broadcast_to(jnp.sum(both[W:], 0, keepdims=True) + mean[j : j + 1], (16, W))
        e_out[j] = e
        l_out[j] = l
        u_out[j : j + 1] = u[0:1]
    nxt[...] = precision[0]
    e_now[...] = e
    l_now[...] = l
    u_now[...] = u

    @pl.when(pl.program_id(0) == pl.num_programs(0) - 1)
    def _():
        packed(e_now[...], l_now[...], u_now[...], total)


def pair_kernel(place, own, other, total, half, after):
    low = place[0] == 0

    @pl.when(low)
    def _():
        after[...] = other[...]
        packed(*composed(unpacked(own), unpacked(other)), total)

    @pl.when(jnp.logical_not(low))
    def _():
        packed(eye(), jnp.zeros((W, W), F32), jnp.zeros((16, W), F32), after)
        packed(*composed(unpacked(other), unpacked(own)), total)

    half[...] = total[pl.ds(pl.multiple_of(place[0] * HALF, 8), HALF), :]


def arrange(core, spot, own, halves, ordered):
    ordered[spot] = own[...]
    mine = pl.multiple_of(core * HALF, 8)
    theirs = pl.multiple_of((1 - core) * HALF, 8)
    for k in range(3):
        slot = lax.rem(spot + k + 1, 4)
        ordered[slot, pl.ds(mine, HALF), :] = halves[2 * k][...]
        ordered[slot, pl.ds(theirs, HALF), :] = halves[2 * k + 1][...]


def quad_kernel(level, place, near, follow, own, *refs):
    halves, (total, half, after, joined, ordered) = refs[:6], refs[6:]
    spot = place[level]
    arrange(place[0], spot, own, halves, ordered)
    parts = [unpacked(ordered.at[k]) for k in range(4)]
    early, late = composed(parts[0], parts[1]), composed(parts[2], parts[3])
    whole = composed(early, late)
    rest = composed(parts[1], late)
    joint = composed(unpacked(near), unpacked(follow))
    packed(*whole, total)
    packed(*joint, joined)
    half[...] = total[pl.ds(pl.multiple_of(place[0] * HALF, 8), HALF), :]
    last = (eye(), jnp.zeros((W, W), F32), jnp.zeros((16, W), F32))
    picked = [
        jnp.where(spot == 0, r, jnp.where(spot == 1, l, jnp.where(spot == 2, p, z)))
        for r, l, p, z in zip(rest, late, parts[3], last)
    ]
    packed(*picked, after)


def finish_kernel(place, near, follow, own, *refs):
    halves, (e_all, l_all, u_all, mean_out, cov_out, ordered, cov_in, mean_in) = refs[:6], refs[6:]

    @pl.when(pl.program_id(0) == 0)
    def _():
        spot = place[3]
        arrange(place[0], spot, own, halves, ordered)
        cov, mean = jnp.zeros((W, W), F32), jnp.zeros((16, W), F32)
        joint = composed(unpacked(near), unpacked(follow))
        _, l, u = unpacked(ordered.at[3])
        cov, mean = jnp.where(spot < 3, l, cov), jnp.where(spot < 3, u, mean)
        for k in (2, 1):
            e, l, u = unpacked(ordered.at[k])
            new_cov, new_mean = applied(split(e), l, u, split(cov), mean)
            cov, mean = jnp.where(spot < k, new_cov, cov), jnp.where(spot < k, new_mean, mean)
        cov_in[...], mean_in[...] = applied(split(joint[0]), joint[1], joint[2], split(cov), mean)

    cov, mean = split(cov_in[...]), mean_in[...]
    for j in range(STEPS):
        now, u = applied(split(e_all[j]), l_all[j], u_all[j : j + 1], cov, mean)
        cov_out[j] = now
        mean_out[j : j + 1] = u[0:1]


def struct(*shape):
    return jax.ShapeDtypeStruct(shape, F32)


def cost(products, passes, size):
    return pl.CostEstimate(
        flops=products * passes * 2 * W**3, bytes_accessed=size, transcendentals=0
    )


PARAMS = pltpu.CompilerParams(vmem_limit_bytes=VMEM_LIMIT)
WHOLE = pl.BlockSpec(memory_space=pltpu.VMEM)
SCALAR = pl.BlockSpec(memory_space=pltpu.SMEM)
ELEMENT = ROWS * 128 * 4


def on_device(filtered_mean, filtered_cov, dynamics, predicted_precision):
    peers = lax.axis_size("tm")
    here = lax.axis_index("tm")
    count = filtered_mean.shape[0]
    blocks = count // STEPS
    matrices = count * W * 256 * 4

    following = lax.ppermute(
        predicted_precision[:1], "tm", [(i, i - 1) for i in range(1, peers)]
    )

    up = lambda i: (i, 0)
    up3 = lambda i: (i, 0, 0)
    vec, mat = pl.BlockSpec((STEPS, W), up), pl.BlockSpec((STEPS, W, W), up3)
    cross, moved = pl.pallas_call(
        cross_kernel,
        grid=(blocks,),
        in_specs=[vec, mat, mat],
        out_specs=[mat, vec],
        out_shape=[struct(count, W, W), struct(count, W)],
        compiler_params=PARAMS,
        cost_estimate=cost(count, 6, 3 * matrices),
        name="cross",
    )(filtered_mean, filtered_cov, dynamics)

    down = pl.BlockSpec((STEPS, W), lambda i: (blocks - 1 - i, 0))
    down3 = pl.BlockSpec((STEPS, W, W), lambda i: (blocks - 1 - i, 0, 0))
    once = pl.BlockSpec((1, W, W), lambda i: (0, 0, 0))
    e_all, l_all, u_all, total = pl.pallas_call(
        fold_kernel,
        grid=(blocks,),
        in_specs=[once, down, down3, down3, down, down3],
        out_specs=[down3, down3, down, pl.BlockSpec((ROWS, 128), lambda i: (0, 0))],
        out_shape=[struct(count, W, W), struct(count, W, W), struct(count, W), struct(ROWS, 128)],
        scratch_shapes=[
            pltpu.VMEM((W, W), F32),
            pltpu.VMEM((W, W), F32),
            pltpu.VMEM((W, W), F32),
            pltpu.VMEM((16, W), F32),
        ],
        compiler_params=PARAMS,
        cost_estimate=cost(5 * count, 6, 5 * matrices),
        name="fold",
    )(following, filtered_mean, filtered_cov, cross, moved, predicted_precision)

    place = jnp.stack(
        [lax.rem(here, 2)] + [lax.rem(lax.div(here, stride), 4) for stride in (2, 8, 32)]
    )

    def other_core(part):
        return lax.ppermute(part, "tm", [(i, i ^ 1) for i in range(peers)])

    total, half, near = pl.pallas_call(
        pair_kernel,
        in_specs=[SCALAR, WHOLE, WHOLE],
        out_specs=[WHOLE] * 3,
        out_shape=[struct(ROWS, 128), struct(HALF, 128), struct(ROWS, 128)],
        compiler_params=PARAMS,
        cost_estimate=cost(3, 3, 4 * ELEMENT),
        name="pair",
    )(place, total, other_core(total))

    def gathered(half, stride, later_only):
        got = [None] * 3
        for k in (2, 1, 3):
            pairs = []
            for i in range(peers):
                spot = i // stride % 4
                if spot + k < 4 or not later_only:
                    pairs.append((i + ((spot + k) % 4 - spot) * stride, i))
            mine = lax.ppermute(half, "tm", pairs)
            got[k - 1] = (mine, other_core(mine))
        return [part for two in got for part in two]

    follow = near
    for level, stride in ((1, 2), (2, 8)):
        parts = gathered(half, stride, False)
        total, half, after, joined = pl.pallas_call(
            functools.partial(quad_kernel, level),
            in_specs=[SCALAR] + [WHOLE] * 9,
            out_specs=[WHOLE] * 4,
            out_shape=[struct(ROWS, 128), struct(HALF, 128), struct(ROWS, 128), struct(ROWS, 128)],
            scratch_shapes=[pltpu.VMEM((4, ROWS, 128), F32)],
            compiler_params=PARAMS,
            cost_estimate=cost(15, 3, 10 * ELEMENT),
            name="quad",
        )(place, near, follow, total, *parts)
        near, follow = (near if stride == 2 else joined), after

    parts = gathered(half, 32, True)
    flat = pl.BlockSpec((ROWS, 128), lambda i: (0, 0))
    flat_half = pl.BlockSpec((HALF, 128), lambda i: (0, 0))
    return pl.pallas_call(
        finish_kernel,
        grid=(blocks,),
        in_specs=[SCALAR] + [flat] * 3 + [flat_half] * 6 + [mat, mat, vec],
        out_specs=[vec, mat],
        out_shape=[struct(count, W), struct(count, W, W)],
        scratch_shapes=[
            pltpu.VMEM((4, ROWS, 128), F32),
            pltpu.VMEM((W, W), F32),
            pltpu.VMEM((16, W), F32),
        ],
        compiler_params=PARAMS,
        cost_estimate=cost(2 * count, 3, 3 * matrices),
        name="finish",
    )(place, near, follow, total, *parts, e_all, l_all, u_all)


def solution(mesh):
    in_specs = (P("tm", None), P("tm", None, None), P("tm", None, None), P("tm", None, None))
    out_specs = (P("tm", None), P("tm", None, None))
    return jax.shard_map(
        lambda *args: tuple(on_device(*args)),
        mesh=mesh,
        in_specs=in_specs,
        out_specs=out_specs,
        check_vma=False,
    )
```

```python
import functools

import jax
import jax.numpy as jnp
from jax import lax
from jax.experimental import pallas as pl
from jax.experimental.pallas import tpu as pltpu
from jax.sharding import PartitionSpec as P

HIGHEST = lax.Precision.HIGHEST
F32 = jnp.float32
W = 192
STEPS = 8
ROWS = 528
HALF = ROWS // 2
VMEM_LIMIT = 60 << 20


def times(a, b):
    return jnp.dot(a, b, precision=HIGHEST, preferred_element_type=F32)


def times_t(a, b):
    return lax.dot_general(
        a, b, (((1,), (1,)), ((), ())), precision=HIGHEST, preferred_element_type=F32
    )


def split(x):
    high = x.astype(jnp.bfloat16)
    return high, (x - high.astype(F32)).astype(jnp.bfloat16)


def filled(x, dim):
    shape = list(x.shape)
    shape[dim] = 256 - W
    return jnp.concatenate([x, jnp.zeros(shape, x.dtype)], dim)


def three(a, b, side):
    high, low = filled(a[0], 1), filled(a[1], 1)
    left = jnp.concatenate([high, high, low], 1)
    high, low = filled(b[0], side), filled(b[1], side)
    right = jnp.concatenate([high, low, high], side)
    return lax.dot_general(left, right, (((1,), (side,)), ((), ())), preferred_element_type=F32)


def packed(e, l, u, ref):
    ref[0:192, :] = e[:, :128]
    ref[192:384, :] = jnp.concatenate([e[:, 128:], l[:, 128:]], 1)
    ref[384:512, :] = l[:128, :128]
    ref[512:528, :] = jnp.zeros((16, 128), F32)
    ref[512:513, :] = u[0:1, :128]
    ref[513:514, 0:64] = u[0:1, 128:]


def unpacked(ref):
    tail = ref[192:384, :]
    e = jnp.concatenate([ref[0:192, :], tail[:, :64]], 1)
    side = tail[:, 64:]
    l = jnp.concatenate([jnp.concatenate([ref[384:512, :], side[:128].T], 0), side], 1)
    u = jnp.concatenate([ref[512:513, :], ref[513:514, 0:64]], 1)
    return e, l, jnp.broadcast_to(u, (16, W))


def applied(e, l, u, cov, mean):
    left = three(e, cov, 0)
    both = three(split(jnp.concatenate([left, mean], 0)), e, 1)
    return both[:W] + l, both[W:] + u


def composed(first, second):
    e = split(first[0])
    l, u = applied(e, first[1], first[2], split(second[1]), second[2])
    return three(e, split(second[0]), 0), l, u


def in_three(rows):
    high = rows.astype(jnp.bfloat16).astype(F32)
    rest = rows - high
    middle = rest.astype(jnp.bfloat16).astype(F32)
    at = lax.broadcasted_iota(jnp.int32, (16, W), 0)
    tail = jnp.where(at == 2, rest - middle, 0.0)
    return jnp.where(at == 0, high, jnp.where(at == 1, middle, tail))


def eye():
    return (
        lax.broadcasted_iota(jnp.int32, (W, W), 0) == lax.broadcasted_iota(jnp.int32, (W, W), 1)
    ).astype(F32)


def cross_kernel(mean, cov, dyn, cross, moved):
    for j in range(STEPS):
        rows = jnp.concatenate([cov[j], jnp.broadcast_to(mean[j : j + 1], (8, W))], 0)
        both = times_t(rows, dyn[j])
        cross[j] = both[:W]
        moved[j : j + 1] = both[W : W + 1]


def fold_kernel(
    following, mean, cov, cross, moved, precision, e_out, l_out, u_out, total, nxt, e_now, l_now, u_now
):
    @pl.when(pl.program_id(0) == 0)
    def _():
        nxt[...] = following[0]
        e_now[...] = eye()
        l_now[...] = jnp.zeros((W, W), F32)
        u_now[...] = jnp.zeros((16, W), F32)

    def element(j):
        after = nxt[...] if j == STEPS - 1 else precision[j + 1]
        gain = times(cross[j], after)
        return gain, cov[j] - times_t(gain, cross[j])

    e, l, u = e_now[...], l_now[...], u_now[...]
    ready = element(STEPS - 1)
    for j in reversed(range(STEPS)):
        gain, resid = ready
        if j:
            ready = element(j - 1)
        gain_split = split(gain)
        left = three(gain_split, split(l), 0)
        e = times(gain, e)
        rows = jnp.concatenate([left, in_three(u - moved[j : j + 1])], 0)
        both = three(split(rows), gain_split, 1)
        l = both[:W] + resid
        u = jnp.broadcast_to(jnp.sum(both[W:], 0, keepdims=True) + mean[j : j + 1], (16, W))
        e_out[j] = e
        l_out[j] = l
        u_out[j : j + 1] = u[0:1]
    nxt[...] = precision[0]
    e_now[...] = e
    l_now[...] = l
    u_now[...] = u

    @pl.when(pl.program_id(0) == pl.num_programs(0) - 1)
    def _():
        packed(e_now[...], l_now[...], u_now[...], total)


def pair_kernel(place, own, other, total, half, after):
    low = place[0] == 0

    @pl.when(low)
    def _():
        after[...] = other[...]
        packed(*composed(unpacked(own), unpacked(other)), total)

    @pl.when(jnp.logical_not(low))
    def _():
        packed(eye(), jnp.zeros((W, W), F32), jnp.zeros((16, W), F32), after)
        packed(*composed(unpacked(other), unpacked(own)), total)

    half[...] = total[pl.ds(pl.multiple_of(place[0] * HALF, 8), HALF), :]


def arrange(core, spot, own, halves, ordered):
    ordered[spot] = own[...]
    mine = pl.multiple_of(core * HALF, 8)
    theirs = pl.multiple_of((1 - core) * HALF, 8)
    for k in range(3):
        slot = lax.rem(spot + k + 1, 4)
        ordered[slot, pl.ds(mine, HALF), :] = halves[2 * k][...]
        ordered[slot, pl.ds(theirs, HALF), :] = halves[2 * k + 1][...]


def quad_kernel(level, place, near, follow, own, *refs):
    halves, (total, half, after, joined, ordered) = refs[:6], refs[6:]
    spot = place[level]
    arrange(place[0], spot, own, halves, ordered)
    parts = [unpacked(ordered.at[k]) for k in range(4)]
    early, late = composed(parts[0], parts[1]), composed(parts[2], parts[3])
    whole = composed(early, late)
    rest = composed(parts[1], late)
    joint = composed(unpacked(near), unpacked(follow))
    packed(*whole, total)
    packed(*joint, joined)
    half[...] = total[pl.ds(pl.multiple_of(place[0] * HALF, 8), HALF), :]
    last = (eye(), jnp.zeros((W, W), F32), jnp.zeros((16, W), F32))
    picked = [
        jnp.where(spot == 0, r, jnp.where(spot == 1, l, jnp.where(spot == 2, p, z)))
        for r, l, p, z in zip(rest, late, parts[3], last)
    ]
    packed(*picked, after)


def finish_kernel(place, near, follow, own, *refs):
    halves, (e_all, l_all, u_all, mean_out, cov_out, ordered, cov_in, mean_in) = refs[:6], refs[6:]

    @pl.when(pl.program_id(0) == 0)
    def _():
        spot = place[3]
        arrange(place[0], spot, own, halves, ordered)
        cov, mean = jnp.zeros((W, W), F32), jnp.zeros((16, W), F32)
        joint = composed(unpacked(near), unpacked(follow))
        _, l, u = unpacked(ordered.at[3])
        cov, mean = jnp.where(spot < 3, l, cov), jnp.where(spot < 3, u, mean)
        for k in (2, 1):
            e, l, u = unpacked(ordered.at[k])
            new_cov, new_mean = applied(split(e), l, u, split(cov), mean)
            cov, mean = jnp.where(spot < k, new_cov, cov), jnp.where(spot < k, new_mean, mean)
        cov_in[...], mean_in[...] = applied(split(joint[0]), joint[1], joint[2], split(cov), mean)

    cov, mean = split(cov_in[...]), mean_in[...]
    for j in range(STEPS):
        now, u = applied(split(e_all[j]), l_all[j], u_all[j : j + 1], cov, mean)
        cov_out[j] = now
        mean_out[j : j + 1] = u[0:1]


def struct(*shape):
    return jax.ShapeDtypeStruct(shape, F32)


def cost(products, passes, size):
    return pl.CostEstimate(
        flops=products * passes * 2 * W**3, bytes_accessed=size, transcendentals=0
    )


PARAMS = pltpu.CompilerParams(vmem_limit_bytes=VMEM_LIMIT)
WHOLE = pl.BlockSpec(memory_space=pltpu.VMEM)
SCALAR = pl.BlockSpec(memory_space=pltpu.SMEM)
ELEMENT = ROWS * 128 * 4


def on_device(filtered_mean, filtered_cov, dynamics, predicted_precision):
    peers = lax.axis_size("tm")
    here = lax.axis_index("tm")
    count = filtered_mean.shape[0]
    blocks = count // STEPS
    matrices = count * W * 256 * 4

    following = lax.ppermute(
        predicted_precision[:1], "tm", [(i, i - 1) for i in range(1, peers)]
    )

    up = lambda i: (i, 0)
    up3 = lambda i: (i, 0, 0)
    vec, mat = pl.BlockSpec((STEPS, W), up), pl.BlockSpec((STEPS, W, W), up3)
    cross, moved = pl.pallas_call(
        cross_kernel,
        grid=(blocks,),
        in_specs=[vec, mat, mat],
        out_specs=[mat, vec],
        out_shape=[struct(count, W, W), struct(count, W)],
        compiler_params=PARAMS,
        cost_estimate=cost(count, 6, 3 * matrices),
        name="cross",
    )(filtered_mean, filtered_cov, dynamics)

    down = pl.BlockSpec((STEPS, W), lambda i: (blocks - 1 - i, 0))
    down3 = pl.BlockSpec((STEPS, W, W), lambda i: (blocks - 1 - i, 0, 0))
    once = pl.BlockSpec((1, W, W), lambda i: (0, 0, 0))
    e_all, l_all, u_all, total = pl.pallas_call(
        fold_kernel,
        grid=(blocks,),
        in_specs=[once, down, down3, down3, down, down3],
        out_specs=[down3, down3, down, pl.BlockSpec((ROWS, 128), lambda i: (0, 0))],
        out_shape=[struct(count, W, W), struct(count, W, W), struct(count, W), struct(ROWS, 128)],
        scratch_shapes=[
            pltpu.VMEM((W, W), F32),
            pltpu.VMEM((W, W), F32),
            pltpu.VMEM((W, W), F32),
            pltpu.VMEM((16, W), F32),
        ],
        compiler_params=PARAMS,
        cost_estimate=cost(5 * count, 6, 5 * matrices),
        name="fold",
    )(following, filtered_mean, filtered_cov, cross, moved, predicted_precision)

    place = jnp.stack(
        [lax.rem(here, 2)] + [lax.rem(lax.div(here, stride), 4) for stride in (2, 8, 32)]
    )

    def other_core(part):
        return lax.ppermute(part, "tm", [(i, i ^ 1) for i in range(peers)])

    total, half, near = pl.pallas_call(
        pair_kernel,
        in_specs=[SCALAR, WHOLE, WHOLE],
        out_specs=[WHOLE] * 3,
        out_shape=[struct(ROWS, 128), struct(HALF, 128), struct(ROWS, 128)],
        compiler_params=PARAMS,
        cost_estimate=cost(3, 3, 4 * ELEMENT),
        name="pair",
    )(place, total, other_core(total))

    def gathered(half, stride, later_only):
        got = [None] * 3
        for k in (2, 1, 3):
            pairs = []
            for i in range(peers):
                spot = i // stride % 4
                if spot + k < 4 or not later_only:
                    pairs.append((i + ((spot + k) % 4 - spot) * stride, i))
            mine = lax.ppermute(half, "tm", pairs)
            got[k - 1] = (mine, other_core(mine))
        return [part for two in got for part in two]

    follow = near
    for level, stride in ((1, 2), (2, 8)):
        parts = gathered(half, stride, False)
        total, half, after, joined = pl.pallas_call(
            functools.partial(quad_kernel, level),
            in_specs=[SCALAR] + [WHOLE] * 9,
            out_specs=[WHOLE] * 4,
            out_shape=[struct(ROWS, 128), struct(HALF, 128), struct(ROWS, 128), struct(ROWS, 128)],
            scratch_shapes=[pltpu.VMEM((4, ROWS, 128), F32)],
            compiler_params=PARAMS,
            cost_estimate=cost(15, 3, 10 * ELEMENT),
            name="quad",
        )(place, near, follow, total, *parts)
        near, follow = (near if stride == 2 else joined), after

    parts = gathered(half, 32, True)
    flat = pl.BlockSpec((ROWS, 128), lambda i: (0, 0))
    flat_half = pl.BlockSpec((HALF, 128), lambda i: (0, 0))
    return pl.pallas_call(
        finish_kernel,
        grid=(blocks,),
        in_specs=[SCALAR] + [flat] * 3 + [flat_half] * 6 + [mat, mat, vec],
        out_specs=[vec, mat],
        out_shape=[struct(count, W), struct(count, W, W)],
        scratch_shapes=[
            pltpu.VMEM((4, ROWS, 128), F32),
            pltpu.VMEM((W, W), F32),
            pltpu.VMEM((16, W), F32),
        ],
        compiler_params=PARAMS,
        cost_estimate=cost(2 * count, 3, 3 * matrices),
        name="finish",
    )(place, near, follow, total, *parts, e_all, l_all, u_all)


def solution(mesh):
    in_specs = (P("tm", None), P("tm", None, None), P("tm", None, None), P("tm", None, None))
    out_specs = (P("tm", None), P("tm", None, None))
    return jax.shard_map(
        lambda *args: tuple(on_device(*args)),
        mesh=mesh,
        in_specs=in_specs,
        out_specs=out_specs,
        check_vma=False,
    )
```
